256 devices in a mesh: dp: 32 (over z, y), expert: 8 (over x, core).
Axes of the slice: x: 4, y: 4, z: 8, core: 2. Of those that a mesh axis runs over, the one named last changes fastest.
Arguments:
- tokens: bfloat16 [1024, 6144], P('expert'), may hold values from -6 to 6
- cotangent: bfloat16 [1024, 6144], P('expert'), may hold values from -6 to 6
- routes: int32 [1024, 2], P('expert'), may hold values from 0 to 7, all different within a row; in each aligned block of 128 rows (0 to 127, 128 to 255, ...) at most 48 rows name the same one
- router_gate_weight: bfloat16 [1024, 2], P('expert'), may hold values from 0.19921875 to 1
- frozen_gate_weight: bfloat16 [8, 6144, 8192], P('expert', None, 'dp'), may hold values from -0.15625 to 0.15625
- frozen_up_weight: bfloat16 [8, 6144, 8192], P('expert', None, 'dp'), may hold values from -0.15625 to 0.15625
- frozen_down_weight: bfloat16 [8, 8192, 6144], P('expert', 'dp'), may hold values from -0.0625 to 0.0625
- gate_adapter_first: bfloat16 [8, 6144, 64], P('expert', 'dp'), may hold values from -0.078125 to 0.078125
- gate_adapter_second: bfloat16 [8, 64, 8192], P('expert', None, 'dp'), may hold values from -0.75 to 0.75
- up_adapter_first: bfloat16 [8, 6144, 64], P('expert', 'dp'), may hold values from -0.078125 to 0.078125
- up_adapter_second: bfloat16 [8, 64, 8192], P('expert', None, 'dp'), may hold values from -0.75 to 0.75
- down_adapter_first: bfloat16 [8, 8192, 64], P('expert', 'dp'), may hold values from -0.0625 to 0.0625
- down_adapter_second: bfloat16 [8, 64, 6144], P('expert', None, 'dp'), may hold values from -0.75 to 0.75
Outputs:
- input_grad: bfloat16 [1024, 6144], P('expert', 'dp')
- gate_grad: float32 [1024, 2], P('expert')
- grad_a_gate: bfloat16 [8, 6144, 64], P('expert', 'dp')
- grad_b_gate: bfloat16 [8, 64, 8192], P('expert', None, 'dp')
- grad_a_up: bfloat16 [8, 6144, 64], P('expert', 'dp')
- grad_b_up: bfloat16 [8, 64, 8192], P('expert', None, 'dp')
- grad_a_down: bfloat16 [8, 8192, 64], P('expert', 'dp')
- grad_b_down: bfloat16 [8, 64, 6144], P('expert', None, 'dp')
The draws below stay inside these ranges and needn't reach their ends.
Inputs may be any that keep to these rules, and one draw needn't show every extreme that they name: `routes`: each token names 2 different experts. Among the 128 tokens of one device no expert is named more than 48 times, a bound that some block reaches.
All inputs are finite; a program needn't handle non-finite values.
Results may differ from the reference program's by a relative error of at most 0.025.
Values may be sent and summed in bfloat16 or wider, within the bound.
No kernel may reach another device: no remote copies, remote signals or barrier semaphores. Data moves between devices by JAX's collectives and lax.ppermute only.
A program may use at most 128 MiB of HBM per device.

```python
import math
import jax
import jax.numpy as jnp
import numpy as np
from jax import lax

HIDDEN_WIDTH = 6144
FEEDFORWARD_HALF = 8192
ADAPTER_RANK = 64
TOP = 2
TOK_DEV = 128
EXPERT_TOTAL = 8
CAP = 48
TOKENS = 1024
N_DP = 32
N_EXPERT = 8


def spiked(result, key, source, target, blocks, factor):
    def block_of(position):
        return (jnp.arange(result.shape[position]) // (result.shape[position] // blocks)).reshape((-1,) + (1,) * (result.ndim - 1 - position))

    near = jax.random.permutation(key, blocks)[block_of(target)]
    other_side = (block_of(target) + blocks // 2) % blocks
    return jnp.where((block_of(source) == near) | (block_of(source) == other_side), factor * result, result)


def block_scale(key, extent, pieces, least, largest):
    gain = 1.0
    for dim, parts in pieces:
        draws = jax.random.uniform(jax.random.fold_in(jax.random.fold_in(key, 6), dim), (parts,), jnp.float32, least / len(pieces), largest / len(pieces))
        gain = gain * jnp.repeat(jnp.exp(draws), extent[dim] // parts).reshape((-1,) + (1,) * (len(extent) - 1 - dim))
    return gain


def deal_out(own_key, own, number, rows, amount, top, most, skew):
    order = jax.random.permutation(own_key, amount)
    crowded, common = shares(amount, rows * top, most, skew, True), shares(amount, rows * top, most, skew, False)
    places = jnp.arange(amount)

    def named(tallies, turn):
        used = int((tallies > 0).sum())
        fixed = max(1, used // 4)
        shifted = fixed + (places - fixed + turn * (used - fixed)) % max(1, amount - fixed)
        return jnp.zeros((amount,), jnp.int32).at[order[jnp.where(places < fixed, places, shifted)]].set(jnp.asarray(tallies, jnp.int32))

    tallies = jnp.where(number % 4 == 0, named(crowded, number // 4), named(common, number - number // 4 - 1))
    mixed = jax.random.permutation(jax.random.fold_in(own, 3), amount)
    source_of, sink = mixed[0:amount // 2 * 2:2], mixed[1:amount // 2 * 2:2]
    slack = jnp.minimum(tallies[source_of] - 1, most - tallies[sink]) // 2
    slack = jnp.where((source_of == order[0]) | (sink == order[0]) | (tallies[sink] == 0), 0, jnp.maximum(slack, 0))
    shifted = jax.random.randint(jax.random.fold_in(own, 4), (amount // 2,), 0, 1 << 20) % (slack + 1)
    tallies = tallies.at[source_of].add(-shifted).at[sink].add(shifted)
    labels = jnp.searchsorted(jnp.cumsum(tallies), jnp.arange(rows * top), side="right").astype(jnp.int32)
    table = labels.reshape(top, rows).T
    table = table[jax.random.permutation(jax.random.fold_in(own, 1), rows)]
    turn = jax.random.randint(jax.random.fold_in(own, 2), (rows, 1), 0, top)
    return jnp.take_along_axis(table, (jnp.arange(top)[None, :] + turn) % top, axis=1)


def shares(number_of, total, most, slope, full):
    loads = [(1 << 20) // math.isqrt(standing ** slope) + 1 for standing in range(1, number_of + 1)]
    largest = most if full else min(most, max(-(-total // number_of), total * loads[0] // sum(loads)))
    least = 1 if total - largest >= number_of - 1 else 0
    counts, spare = [largest] + [least] * (number_of - 1), total - largest - least * (number_of - 1)
    while spare > 0:
        movable = [i for i in range(1, number_of) if counts[i] < largest] or [i for i in range(1, number_of) if counts[i] < most]
        pool, budget = sum([loads[i] for i in movable]), spare
        for i in movable:
            more = min(most - counts[i], max(1, budget * loads[i] // pool), spare)
            counts[i] = counts[i] + more
            spare = spare - more
    return np.array(counts)


def gaussian(rng, dims, scale, reach, pieces=(), kind=jnp.bfloat16):
    gain = block_scale(rng, dims, pieces, -0.22, 0.18) if pieces else 1.0
    drawn = jax.random.normal(rng, dims, jnp.float32) * scale * gain
    return jnp.minimum(jnp.maximum(drawn, -reach), reach).astype(kind)


def bell_draw_with(key, shape, width, bound, pieces, heavy, kind=jnp.bfloat16):
    result = width * jax.random.normal(key, shape, jnp.float32)
    if pieces:
        result = result * block_scale(key, shape, pieces, -0.22, 0.18)
    return jnp.clip(spiked(result, jax.random.fold_in(key, 3), *heavy), -bound, bound).astype(kind)


def setup_inputs(seed: int = 0) -> dict:
    key_of = jax.random.split(jax.random.key(seed), 14)
    tokens = gaussian(key_of[0], (TOKENS, HIDDEN_WIDTH), 1.0, 6.0, ((0, 8),))
    cotangent = gaussian(key_of[1], (TOKENS, HIDDEN_WIDTH), 1.0, 6.0, ((0, 8),))
    routes_keys = jax.random.split(jax.random.fold_in(key_of[2], 1), TOKENS // TOK_DEV)
    routes_turns = jax.random.permutation(jax.random.fold_in(key_of[2], 3), TOKENS // TOK_DEV)
    routes = jax.vmap(lambda own, number: deal_out(jax.random.fold_in(key_of[2], 2), own, number, TOK_DEV, EXPERT_TOTAL, TOP, CAP, 2))(routes_keys, routes_turns).reshape((TOKENS, TOP))
    router_gate_weight = jnp.clip(0.19921875 + 0.80078125 * jax.random.uniform(key_of[3], (TOKENS, TOP), jnp.float32) ** block_scale(key_of[3], (TOKENS, TOP), ((0, 8),), -0.2, 0.2), 0.19921875, 1.0).astype(jnp.bfloat16)
    frozen_gate_weight = bell_draw_with(key_of[4], (EXPERT_TOTAL, HIDDEN_WIDTH, FEEDFORWARD_HALF), HIDDEN_WIDTH ** -0.5, 0.15625, ((0, 8), (2, 32)), (2, 1, 32, 2.75))
    frozen_up_weight = bell_draw_with(key_of[5], (EXPERT_TOTAL, HIDDEN_WIDTH, FEEDFORWARD_HALF), HIDDEN_WIDTH ** -0.5, 0.15625, ((0, 8), (2, 32)), (2, 1, 32, 2.75))
    frozen_down_weight = gaussian(key_of[6], (EXPERT_TOTAL, FEEDFORWARD_HALF, HIDDEN_WIDTH), FEEDFORWARD_HALF ** -0.5, 0.0625, ((0, 8), (1, 32)))
    gate_adapter_first = gaussian(key_of[7], (EXPERT_TOTAL, HIDDEN_WIDTH, ADAPTER_RANK), HIDDEN_WIDTH ** -0.5, 0.078125, ((0, 8), (1, 32)))
    gate_adapter_second = gaussian(key_of[8], (EXPERT_TOTAL, ADAPTER_RANK, FEEDFORWARD_HALF), ADAPTER_RANK ** -0.5, 0.75, ((0, 8), (2, 32)))
    up_adapter_first = gaussian(key_of[9], (EXPERT_TOTAL, HIDDEN_WIDTH, ADAPTER_RANK), HIDDEN_WIDTH ** -0.5, 0.078125, ((0, 8), (1, 32)))
    up_adapter_second = gaussian(key_of[10], (EXPERT_TOTAL, ADAPTER_RANK, FEEDFORWARD_HALF), ADAPTER_RANK ** -0.5, 0.75, ((0, 8), (2, 32)))
    down_adapter_first = gaussian(key_of[11], (EXPERT_TOTAL, FEEDFORWARD_HALF, ADAPTER_RANK), FEEDFORWARD_HALF ** -0.5, 0.0625, ((0, 8), (1, 32)))
    down_adapter_second = gaussian(key_of[12], (EXPERT_TOTAL, ADAPTER_RANK, HIDDEN_WIDTH), ADAPTER_RANK ** -0.5, 0.75, ((0, 8), (2, 32)))
    return dict(tokens=tokens, cotangent=cotangent, routes=routes, router_gate_weight=router_gate_weight, frozen_gate_weight=frozen_gate_weight, frozen_up_weight=frozen_up_weight, frozen_down_weight=frozen_down_weight, gate_adapter_first=gate_adapter_first, gate_adapter_second=gate_adapter_second, up_adapter_first=up_adapter_first, up_adapter_second=up_adapter_second, down_adapter_first=down_adapter_first, down_adapter_second=down_adapter_second)


adapter_scale = 0.25
highest = lax.Precision.HIGHEST


def contract_matrices(former, latter, dim_one, dim_two, strict):
    setting = highest if strict else None
    return lax.dot_general(former, latter, (((dim_one,), (dim_two,)), ((), ())), precision=setting, preferred_element_type=jnp.float32)


def reference(tokens, cotangent, routes, router_gate_weight, frozen_gate_weight, frozen_up_weight, frozen_down_weight, gate_adapter_first, gate_adapter_second, up_adapter_first, up_adapter_second, down_adapter_first, down_adapter_second):
    slot_count = N_EXPERT * CAP
    ff_block = FEEDFORWARD_HALF // N_DP
    flat_routes = routes.reshape(-1)
    flat_gates = router_gate_weight.reshape(-1).astype(jnp.float32)

    def per_expert(running, stacked):
        dx_total, score_total = running
        expert = stacked[0]
        gate_weight_slice, up_weight_slice, weight_down, gate_first_factor, gate_second_factor, up_first_factor, up_second_factor, down_first_factor, down_second_factor = stacked[1:]
        chosen = flat_routes == expert
        picked = jnp.nonzero(chosen, size=slot_count, fill_value=0)[0].astype(jnp.int32)
        usable = (jnp.arange(slot_count, dtype=jnp.int32) < jnp.sum(chosen.astype(jnp.int32))).astype(jnp.float32)
        token_ids = (picked // TOP).astype(jnp.int32)
        router_weighting = flat_gates[picked] * usable
        input_rows = tokens[token_ids]
        output_gradient_rows = cotangent[token_ids]
        gate_lowrank_product = contract_matrices(input_rows, gate_first_factor, 1, 0, False).astype(jnp.bfloat16)
        up_lowrank_product = contract_matrices(input_rows, up_first_factor, 1, 0, False).astype(jnp.bfloat16)
        gate_preactivation = contract_matrices(input_rows, gate_weight_slice, 1, 0, False) + adapter_scale * contract_matrices(gate_lowrank_product, gate_second_factor, 1, 0, False)
        up_preactivation = contract_matrices(input_rows, up_weight_slice, 1, 0, False) + adapter_scale * contract_matrices(up_lowrank_product, up_second_factor, 1, 0, False)
        sigmoid_gate = jax.nn.sigmoid(gate_preactivation)
        swish_gate = gate_preactivation * sigmoid_gate
        hidden_activation = (swish_gate * up_preactivation).astype(jnp.bfloat16)
        backward_projection = contract_matrices(output_gradient_rows, weight_down, 1, 1, False)
        lookup_complete = contract_matrices(output_gradient_rows, down_second_factor, 1, 1, False)
        lookup_lowrank = lookup_complete.astype(jnp.bfloat16)
        hidden_activation_gradient = router_weighting[:, None] * (backward_projection + adapter_scale * contract_matrices(lookup_lowrank, down_first_factor, 1, 1, False))
        slope_gate = sigmoid_gate * (1.0 + gate_preactivation * (1.0 - sigmoid_gate))
        gate_branch_gradient = (hidden_activation_gradient * up_preactivation * slope_gate).astype(jnp.bfloat16)
        up_branch_gradient = (hidden_activation_gradient * swish_gate).astype(jnp.bfloat16)
        gate_adapter_branch = contract_matrices(gate_branch_gradient, gate_second_factor, 1, 1, False)
        up_adapter_branch = contract_matrices(up_branch_gradient, up_second_factor, 1, 1, False)
        down_adapter_branch = contract_matrices(hidden_activation, down_first_factor, 1, 0, False)
        router_score_rows = jnp.sum(backward_projection * hidden_activation.astype(jnp.float32), axis=1) + adapter_scale * jnp.sum(lookup_complete * down_adapter_branch, axis=1)

        def block_term(total, block):
            start = block * ff_block
            grad_g = lax.dynamic_slice_in_dim(gate_branch_gradient, start, ff_block, 1)
            grad_u = lax.dynamic_slice_in_dim(up_branch_gradient, start, ff_block, 1)
            piece_g = lax.dynamic_slice_in_dim(gate_weight_slice, start, ff_block, 1)
            piece_u = lax.dynamic_slice_in_dim(up_weight_slice, start, ff_block, 1)
            term = contract_matrices(grad_g, piece_g, 1, 1, False) + contract_matrices(grad_u, piece_u, 1, 1, False)
            return total + lax.optimization_barrier(term.astype(jnp.bfloat16)).astype(jnp.float32), None

        frozen_input_gradient, _ = lax.scan(block_term, jnp.zeros((slot_count, HIDDEN_WIDTH), jnp.float32), jnp.arange(N_DP, dtype=jnp.int32))
        complete_input_gradient = frozen_input_gradient + adapter_scale * (contract_matrices(gate_adapter_branch, gate_first_factor.astype(jnp.float32), 1, 1, True) + contract_matrices(up_adapter_branch, up_first_factor.astype(jnp.float32), 1, 1, True))
        input_broadcast = input_rows.astype(jnp.float32)
        gate_first_partial = adapter_scale * contract_matrices(input_broadcast, gate_adapter_branch, 0, 0, True)
        up_first_partial = adapter_scale * contract_matrices(input_broadcast, up_adapter_branch, 0, 0, True)
        gate_second_partial = adapter_scale * contract_matrices(gate_lowrank_product, gate_branch_gradient, 0, 0, False)
        up_second_partial = adapter_scale * contract_matrices(up_lowrank_product, up_branch_gradient, 0, 0, False)
        down_first_partial = adapter_scale * contract_matrices(hidden_activation.astype(jnp.float32), router_weighting[:, None] * lookup_complete, 0, 0, True)
        down_second_partial = adapter_scale * contract_matrices(router_weighting[:, None] * down_adapter_branch, output_gradient_rows.astype(jnp.float32), 0, 0, True)
        dx_total = dx_total.at[token_ids].add(complete_input_gradient)
        score_total = score_total.at[picked].add(router_score_rows * usable)
        return (dx_total, score_total), (gate_first_partial, gate_second_partial, up_first_partial, up_second_partial, down_first_partial, down_second_partial)

    start_state = (jnp.zeros((TOKENS, HIDDEN_WIDTH), jnp.float32), jnp.zeros((TOKENS * TOP,), jnp.float32))
    stacked_gradients = (jnp.arange(EXPERT_TOTAL, dtype=jnp.int32), frozen_gate_weight, frozen_up_weight, frozen_down_weight, gate_adapter_first, gate_adapter_second, up_adapter_first, up_adapter_second, down_adapter_first, down_adapter_second)
    final_state, grads = lax.scan(per_expert, start_state, stacked_gradients)
    dx_total, score_total = final_state
    gate_first_gradient, gate_second_gradient, up_first_gradient, up_second_gradient, down_first_gradient, down_second_gradient = grads
    return (dx_total.astype(jnp.bfloat16), score_total.reshape(TOKENS, TOP),
            gate_first_gradient.astype(jnp.bfloat16), gate_second_gradient.astype(jnp.bfloat16),
            up_first_gradient.astype(jnp.bfloat16), up_second_gradient.astype(jnp.bfloat16),
            down_first_gradient.astype(jnp.bfloat16), down_second_gradient.astype(jnp.bfloat16))
```

```python
import jax
import jax.numpy as jnp
from jax import lax
from jax.sharding import PartitionSpec as P

NZ, NY, NX, NC = 8, 4, 4, 2
SCALE = 0.25
CAP = 48
GRP = 2 * CAP
Y_BASE, Y_WIDE = 0, 768
Z_BASE, Z_WIDE = 3072, 256
D_BASE, D_WIDE = 5120, 1024
HALF = 96
bf16 = jnp.bfloat16
f32 = jnp.float32


def z_perm(s):
    return [(z * NY + y, ((z + s) % NZ) * NY + y) for z in range(NZ) for y in range(NY)]


def y_perm(s):
    return [(z * NY + y, z * NY + (y + s) % NY) for z in range(NZ) for y in range(NY)]


def x_perm(s):
    return [(x * NC + c, ((x + s) % NX) * NC + c) for x in range(NX) for c in range(NC)]


CORE = [(x * NC + c, x * NC + 1 - c) for x in range(NX) for c in range(NC)]


def over_dp(a, perm):
    return lax.ppermute(a, "dp", perm)


def over_expert(a, perm):
    return lax.ppermute(a, "expert", perm)


def dot(a, b, i, j):
    return lax.dot_general(a, b, (((i,), (j,)), ((), ())), preferred_element_type=f32)


def ring_gather(own, perm, n):
    got = {0: own}
    fore, aft = own, own
    for k in range(1, n // 2):
        fore = over_dp(fore, perm(1))
        aft = over_dp(aft, perm(-1))
        got[-k] = fore
        got[k] = aft
    half = own.shape[0] // 2
    top = over_dp(fore[:half], perm(1))
    bottom = over_dp(aft[half:], perm(-1))
    got[n // 2] = jnp.concatenate([top, bottom], axis=0)
    return got


def ring_scatter(term, perm, n):
    far = term(n // 2).astype(bf16)
    half = far.shape[0] // 2
    fore = over_dp(far[:half], perm(1))
    aft = over_dp(far[half:], perm(-1))
    for k in range(n // 2 - 1, 0, -1):
        up, down = term(k), term(-k)
        if k == n // 2 - 1:
            up = jnp.concatenate([up[:half] + fore.astype(f32), up[half:]], axis=0)
            down = jnp.concatenate([down[:half], down[half:] + aft.astype(f32)], axis=0)
        else:
            up = up + fore.astype(f32)
            down = down + aft.astype(f32)
        fore = over_dp(up.astype(bf16), perm(1))
        aft = over_dp(down.astype(bf16), perm(-1))
    return term(0) + fore.astype(f32) + aft.astype(f32)


def small_sum(part):
    n = NZ * NY
    rows, wide = part.shape
    split = part.astype(bf16).reshape(n, rows // n, wide)
    mine = lax.all_to_all(split, "dp", split_axis=0, concat_axis=0, tiled=True)
    mine = jnp.sum(mine.astype(f32), axis=0).astype(bf16)
    spread = jnp.broadcast_to(mine[None], (n, rows // n, wide))
    full = lax.all_to_all(spread, "dp", split_axis=0, concat_axis=0, tiled=True)
    return full.reshape(rows, wide)


def body(
    tokens,
    cotangent,
    routes,
    router_gate_weight,
    frozen_gate_weight,
    frozen_up_weight,
    frozen_down_weight,
    gate_adapter_first,
    gate_adapter_second,
    up_adapter_first,
    up_adapter_second,
    down_adapter_first,
    down_adapter_second,
):
    d = lax.axis_index("dp")
    e = lax.axis_index("expert")
    z, y = d // NY, d % NY
    x, c = e // NC, e % NC
    rows_dev = tokens.shape[0]
    wg, wu, wd = frozen_gate_weight[0], frozen_up_weight[0], frozen_down_weight[0]
    a_gate, a_up, d_second = gate_adapter_first[0], up_adapter_first[0], down_adapter_second[0]
    b_gate, b_up, d_first = gate_adapter_second[0], up_adapter_second[0], down_adapter_first[0]

    info = jnp.concatenate([routes.astype(f32), router_gate_weight.astype(f32)], axis=1)
    info = jnp.concatenate([info, over_expert(info, CORE)], axis=0)
    tok = jnp.concatenate([tokens, over_expert(tokens, CORE)], axis=0)
    cot = jnp.concatenate([cotangent, over_expert(cotangent, CORE)], axis=0)

    lane = jnp.arange(NX * GRP, dtype=jnp.int32)[None, :]
    row = jnp.arange(2 * rows_dev, dtype=jnp.int32)[:, None]
    expert = (2 * ((x + lane // GRP) % NX) + c).astype(f32)
    in_block = (row // rows_dev) == ((lane // CAP) % 2)
    first = (info[:, 0:1] == expert) & in_block
    second = (info[:, 1:2] == expert) & in_block
    either = (first | second).astype(bf16)
    earlier = (row.T < row).astype(bf16)
    rank = dot(earlier, either, 1, 0)
    placed = rank == (lane % CAP).astype(f32)
    first = (first & placed).astype(f32)
    second = (second & placed).astype(f32)
    place = (first + second).astype(bf16)
    weighted = (first * info[:, 2:3] + second * info[:, 3:4]).astype(bf16)

    def rows_of(which, start, wide, lo, hi):
        src = tok if which == 0 else cot
        sel = place if which == 0 else weighted
        cols = lax.dynamic_slice_in_dim(src, start, wide, 1)
        return dot(sel[:, lo:hi], cols, 0, 0).astype(bf16)

    own_start = d * 192
    z_start = Z_BASE + z * Z_WIDE
    y_start = Y_BASE + y * Y_WIDE

    def exchange(parts):
        got = [
            [over_expert(p[(r - 1) * GRP : r * GRP], x_perm(r)) for r in (1, 2, 3)] for p in parts
        ]
        return [jnp.concatenate(g, axis=0) for g in got]

    far = NX * GRP
    z_msg = jnp.concatenate(
        [rows_of(0, z_start, Z_WIDE, GRP, far), rows_of(1, z_start, Z_WIDE, GRP, far)]
        + [rows_of(0, own_start, 192, GRP, far), rows_of(1, own_start, 192, GRP, far)],
        axis=1,
    )
    y_msg = jnp.concatenate(
        [rows_of(0, y_start, Y_WIDE, GRP, far), rows_of(1, y_start, Y_WIDE, GRP, far)], axis=1
    )
    d_msg = jnp.concatenate(
        [rows_of(0, D_BASE, D_WIDE, GRP, far), rows_of(1, D_BASE, D_WIDE, GRP, far)], axis=1
    )
    (z_got,) = exchange([z_msg])
    (y_got,) = exchange([y_msg])
    (d_got,) = exchange([d_msg])
    x_near = rows_of(0, 0, tok.shape[1], 0, GRP)
    dy_near = rows_of(1, 0, cot.shape[1], 0, GRP)

    z_all = ring_gather(z_got[:, : 2 * Z_WIDE], z_perm, NZ)
    y_all = ring_gather(y_got, y_perm, NY)

    own = z_got[:, 2 * Z_WIDE :]
    x_own = jnp.concatenate([lax.dynamic_slice_in_dim(x_near, own_start, 192, 1), own[:, :192]], 0)
    dy_own = jnp.concatenate(
        [lax.dynamic_slice_in_dim(dy_near, own_start, 192, 1), own[:, 192:]], 0
    )
    low = small_sum(
        jnp.concatenate(
            [dot(x_own, a_gate, 1, 0), dot(x_own, a_up, 1, 0), dot(dy_own, d_second, 1, 1)], axis=1
        )
    )

    def add_chunk(total, chunk, start, wide):
        xs, dys = chunk[:, :wide], chunk[:, wide:]
        g = dot(xs, lax.dynamic_slice_in_dim(wg, start, wide, 0), 1, 0)
        u = dot(xs, lax.dynamic_slice_in_dim(wu, start, wide, 0), 1, 0)
        b = dot(dys, lax.dynamic_slice_in_dim(wd, start, wide, 1), 1, 1)
        if total is None:
            return g, u, b
        return total[0] + g, total[1] + u, total[2] + b

    total = None
    for k, chunk in z_all.items():
        total = add_chunk(total, chunk, Z_BASE + ((z + k) % NZ) * Z_WIDE, Z_WIDE)
    for k, chunk in y_all.items():
        total = add_chunk(total, chunk, Y_BASE + ((y + k) % NY) * Y_WIDE, Y_WIDE)
    total = add_chunk(total, d_got, D_BASE, D_WIDE)
    near = (dot(x_near, wg, 1, 0), dot(x_near, wu, 1, 0), dot(dy_near, wd, 1, 1))
    gate_in, up_in, back = (jnp.concatenate([n, t], axis=0) for n, t in zip(near, total))

    low_gate, low_up, query = low[:, :64], low[:, 64:128], low[:, 128:]
    gate_pre = gate_in + SCALE * dot(low_gate, b_gate, 1, 0)
    up_pre = up_in + SCALE * dot(low_up, b_up, 1, 0)
    sig = jax.nn.sigmoid(gate_pre)
    swish = gate_pre * sig
    hidden = (swish * up_pre).astype(bf16)
    grad_hidden = back + SCALE * dot(query, d_first, 1, 1)
    grad_gate = (grad_hidden * up_pre * (sig * (1.0 + gate_pre * (1.0 - sig)))).astype(bf16)
    grad_up = (grad_hidden * swish).astype(bf16)
    side_down = dot(hidden, d_first, 1, 0)
    score = jnp.sum(back * hidden.astype(f32), axis=1) + SCALE * jnp.sum(
        query.astype(f32) * side_down, axis=1
    )
    sides = small_sum(
        jnp.concatenate(
            [dot(grad_gate, b_gate, 1, 1), dot(grad_up, b_up, 1, 1), side_down, score[:, None]],
            axis=1,
        )
    )
    both_sides, side_down = sides[:, :128], sides[:, 128:192]

    wg4 = wg.reshape(NZ, NY, 192, wg.shape[1])
    wu4 = wu.reshape(NZ, NY, 192, wu.shape[1])

    def y_term(k):
        i = (y + k) % NY
        pick = lambda w: lax.dynamic_slice_in_dim(w[:, :, :HALF], i, 1, 1).reshape(NZ * HALF, -1)
        return dot(pick(wg4), grad_gate, 1, 1) + dot(pick(wu4), grad_up, 1, 1)

    def z_term(k):
        i = (z + k) % NZ
        pick = lambda w: lax.dynamic_slice_in_dim(w[:, :, HALF:], i, 1, 0).reshape(NY * HALF, -1)
        return dot(pick(wg4), grad_gate, 1, 1) + dot(pick(wu4), grad_up, 1, 1)

    after_y = ring_scatter(y_term, y_perm, NY).astype(bf16).reshape(NZ, HALF, -1)
    after_z = ring_scatter(z_term, z_perm, NZ).astype(bf16).reshape(NY, HALF, -1)
    take = lambda a, i: lax.dynamic_index_in_dim(a, i, 0, keepdims=False).astype(f32)
    upper = ring_scatter(lambda k: take(after_y, (z + k) % NZ), z_perm, NZ)
    lower = ring_scatter(lambda k: take(after_z, (y + k) % NY), y_perm, NY)
    a_both = jnp.concatenate([a_gate, a_up], axis=1)
    summed = jnp.concatenate([upper, lower], axis=0) + SCALE * dot(a_both, both_sides, 1, 1)
    final = jnp.concatenate(
        [summed.astype(bf16), jnp.broadcast_to(sides[:, 192][None], (16, far))], axis=0
    )
    parts = [final[:, :GRP]] + [
        over_expert(final[:, r * GRP : (r + 1) * GRP], x_perm(-r)) for r in (1, 2, 3)
    ]
    final = jnp.concatenate(parts, axis=1)
    out = dot(place, final[:192], 1, 1)
    scores = final[192:193].astype(f32)
    out = jnp.concatenate(
        [
            out,
            jnp.sum(first * scores, axis=1, keepdims=True),
            jnp.sum(second * scores, axis=1, keepdims=True),
        ],
        axis=1,
    )
    out = out[:rows_dev] + over_expert(out[rows_dev:], CORE)
    input_grad = out[:, :192].astype(bf16)
    gate_grad = out[:, 192:194] / router_gate_weight.astype(f32)

    grad_a_gate = SCALE * dot(x_own, both_sides[:, :64], 0, 0)
    grad_a_up = SCALE * dot(x_own, both_sides[:, 64:], 0, 0)
    grad_b_gate = SCALE * dot(low_gate, grad_gate, 0, 0)
    grad_b_up = SCALE * dot(low_up, grad_up, 0, 0)
    grad_a_down = SCALE * dot(hidden, query, 0, 0)
    grad_b_down = SCALE * dot(side_down, dy_own, 0, 0)
    return (
        input_grad,
        gate_grad,
        grad_a_gate.astype(bf16)[None],
        grad_b_gate.astype(bf16)[None],
        grad_a_up.astype(bf16)[None],
        grad_b_up.astype(bf16)[None],
        grad_a_down.astype(bf16)[None],
        grad_b_down.astype(bf16)[None],
    )


def solution(mesh):
    return jax.shard_map(
        body,
        mesh=mesh,
        in_specs=(
            P("expert", None),
            P("expert", None),
            P("expert", None),
            P("expert", None),
            P("expert", None, "dp"),
            P("expert", None, "dp"),
            P("expert", "dp", None),
            P("expert", "dp", None),
            P("expert", None, "dp"),
            P("expert", "dp", None),
            P("expert", None, "dp"),
            P("expert", "dp", None),
            P("expert", None, "dp"),
        ),
        out_specs=(
            P("expert", "dp"),
            P("expert", None),
            P("expert", "dp", None),
            P("expert", None, "dp"),
            P("expert", "dp", None),
            P("expert", None, "dp"),
            P("expert", "dp", None),
            P("expert", None, "dp"),
        ),
        check_vma=False,
    )
```

```python
import functools

import jax
import jax.numpy as jnp
from jax import lax
from jax.experimental import pallas as pl
from jax.experimental.pallas import tpu as pltpu
from jax.sharding import PartitionSpec as P

NZ, NY, NX, NC = 8, 4, 4, 2
SCALE = 0.25
CAP = 48
GRP = 2 * CAP
Y_BASE, Y_WIDE = 0, 896
D_BASE, D_WIDE = 3584, 2560
HALF = 96
bf16 = jnp.bfloat16
f32 = jnp.float32


def z_perm(s):
    return [(z * NY + y, ((z + s) % NZ) * NY + y) for z in range(NZ) for y in range(NY)]


def y_perm(s):
    return [(z * NY + y, z * NY + (y + s) % NY) for z in range(NZ) for y in range(NY)]


def x_perm(s):
    return [(x * NC + c, ((x + s) % NX) * NC + c) for x in range(NX) for c in range(NC)]


CORE = [(x * NC + c, x * NC + 1 - c) for x in range(NX) for c in range(NC)]


def over_dp(a, perm):
    return lax.ppermute(a, "dp", perm)


def over_expert(a, perm):
    return lax.ppermute(a, "expert", perm)


def dot(a, b, i, j):
    return lax.dot_general(a, b, (((i,), (j,)), ((), ())), preferred_element_type=f32)


MIB = 1024 * 1024
BIG = 58 * MIB
OWN_AT = 2 * Y_WIDE
ROWS = NX * GRP
FAR = ROWS - GRP
FF = 256
VMEM = pltpu.VMEM
ANY = pl.BlockSpec(memory_space=pl.ANY)
INV = pl.BlockSpec(memory_space=pltpu.VMEM)
INS = pl.BlockSpec(memory_space=pltpu.SMEM)


def shape(dims, kind=bf16):
    return jax.ShapeDtypeStruct(dims, kind)


def lanes(ref, start, wide):
    return ref[:, pl.ds(pl.multiple_of(start, 128), wide)]


def fetch(pairs, sem):
    copies = [pltpu.make_async_copy(a, b, sem.at[i]) for i, (a, b) in enumerate(pairs)]
    for copy in copies:
        copy.start()
    return copies


def slot_rows(sel, own, partner, cols):
    src = jnp.concatenate([own[:, cols], partner[:, cols]], axis=0)
    return jnp.dot(sel, src, preferred_element_type=f32)


def put(refs, at, value):
    value = value.astype(bf16)
    for r in range(3):
        refs[r][:, at : at + value.shape[1]] = value[r * GRP : (r + 1) * GRP]


def place_kernel(pos, info, info_p, tok, tok_p, cot, cot_p, *outs):
    ring_out, d_out = outs[0:3], outs[3:6]
    near_x, near_dy, near_own, place_out, first_out = outs[6:11]
    y_cols, own_cols, wholes, sem = outs[11:15], outs[15:19], outs[19:23], outs[23]
    d, y = pos[0], pos[2]
    odd = d % 2
    y_at = pl.ds(pl.multiple_of(Y_BASE + y * Y_WIDE, 128), Y_WIDE)
    own_at = pl.ds(pl.multiple_of(192 * d - 64 * odd, 128), 256)
    srcs = (tok, tok_p, cot, cot_p)
    copies = fetch(
        [(a.at[:, y_at], b) for a, b in zip(srcs, y_cols)]
        + [(a.at[:, own_at], b) for a, b in zip(srcs, own_cols)]
        + list(zip(srcs, wholes)),
        sem,
    )
    n = tok.shape[0]
    info_all = jnp.concatenate([info[...], info_p[...]], axis=1)
    lane = lax.broadcasted_iota(jnp.int32, (ROWS, 2 * n), 0)
    group = jnp.zeros((ROWS, 2 * n), jnp.int32)
    for k in range(1, NX * NC):
        group = group + jnp.where(lane >= k * CAP, 1, 0)
    slot = (lane - CAP * group).astype(f32)
    block = (group & 1).astype(f32)
    expert = (2 * ((pos[3] + (group >> 1)) & (NX - 1)) + pos[4]).astype(f32)
    ones = jnp.ones((ROWS, 2 * n), f32)
    zeros = jnp.zeros((ROWS, 2 * n), f32)
    token = lax.broadcasted_iota(jnp.int32, (ROWS, 2 * n), 1)
    mine = jnp.where(jnp.where(token >= n, ones, zeros) == block, ones, zeros)
    first = jnp.where(info_all[0:1] == expert, mine, zeros)
    second = jnp.where(info_all[1:2] == expert, mine, zeros)
    row = lax.broadcasted_iota(jnp.int32, (2 * n, 2 * n), 0)
    col = lax.broadcasted_iota(jnp.int32, (2 * n, 2 * n), 1)
    earlier = jnp.where(row < col, 1.0, 0.0).astype(bf16)
    rank = jnp.dot((first + second).astype(bf16), earlier, preferred_element_type=f32)
    first = jnp.where(rank == slot, first, zeros)
    second = jnp.where(rank == slot, second, zeros)
    place = (first + second).astype(bf16)
    weighted = (first * info_all[2:3] + second * info_all[3:4]).astype(bf16)
    place_out[...] = place
    first_out[...] = first.astype(bf16)
    for copy in copies[:8]:
        copy.wait()
    every = slice(None)
    put(ring_out, 0, slot_rows(place[GRP:], y_cols[0], y_cols[1], every))
    put(ring_out, Y_WIDE, slot_rows(weighted[GRP:], y_cols[2], y_cols[3], every))
    for i, sel in enumerate((place, weighted)):
        v = slot_rows(sel, own_cols[2 * i], own_cols[2 * i + 1], every)
        v = jnp.where(odd == 1, pltpu.roll(v, 192, 1), v)
        near_own[:, 256 * i : 256 * i + 256] = v[:GRP].astype(bf16)
        put(d_out, 2 * D_WIDE + 256 * i, v[GRP:])
    for copy in copies[8:]:
        copy.wait()
    step = 512
    for i in range(tok.shape[1] // step):
        cols = slice(i * step, (i + 1) * step)
        for j, (sel, near) in enumerate(((place, near_x), (weighted, near_dy))):
            whole = i * step >= D_BASE
            v = slot_rows(sel if whole else sel[:GRP], wholes[2 * j], wholes[2 * j + 1], cols)
            near[:, cols] = v[:GRP].astype(bf16)
            if whole:
                put(d_out, i * step - D_BASE + j * D_WIDE, v[GRP:])


def place_rows(pos, info, info_p, tok, tok_p, cot, cot_p):
    n = tok.shape[0]
    out = [shape((GRP, OWN_AT))] * 3 + [shape((GRP, 2 * D_WIDE + 512))] * 3
    out += [shape((GRP, tok.shape[1]))] * 2 + [shape((GRP, 512))] + [shape((ROWS, 256))] * 2
    return pl.pallas_call(
        place_kernel,
        out_shape=out,
        in_specs=[INS] + [INV] * 2 + [ANY] * 4,
        out_specs=[INV] * len(out),
        scratch_shapes=[VMEM((n, Y_WIDE), bf16)] * 4
        + [VMEM((n, 256), bf16)] * 4
        + [VMEM(tok.shape, bf16)] * 4
        + [pltpu.SemaphoreType.DMA((12,))],
        compiler_params=pltpu.CompilerParams(vmem_limit_bytes=BIG),
        name="place_rows",
    )(pos, info, info_p, tok, tok_p, cot, cot_p)


def nt(a, b):
    return lax.dot_general(a, b, (((1,), (1,)), ((), ())), preferred_element_type=f32)


def nn(a, b):
    return jnp.dot(a, b, preferred_element_type=f32)


def start_of(pos, kind, k):
    if kind == "y":
        return Y_BASE + ((pos[2] + k + NY) % NY) * Y_WIDE, Y_WIDE
    return D_BASE, D_WIDE


def join_kernel(m1, m2, m3, d1, d2, d3, y_out, o1, o2, o3):
    for r, (m, d, o) in enumerate(((m1, d1, o1), (m2, d2, o2), (m3, d3, o3))):
        y_out[r * GRP : (r + 1) * GRP] = m[...]
        o[...] = d[...]


def join_rows(messages, later):
    return pl.pallas_call(
        join_kernel,
        out_shape=[shape((FAR, OWN_AT))] + [shape(a.shape) for a in later],
        in_specs=[INV] * 6,
        out_specs=[INV] * 4,
        compiler_params=pltpu.CompilerParams(vmem_limit_bytes=BIG),
        name="join_rows",
    )(*messages, *later)


def spread_kernel(a, after, out):
    total = jnp.sum(a[...].astype(f32), axis=0).astype(bf16)
    for k in range(out.shape[0]):
        out[k] = total


def spread_sum(a, after):
    return pl.pallas_call(
        spread_kernel,
        out_shape=shape(a.shape),
        in_specs=[INV, ANY],
        out_specs=INV,
        compiler_params=pltpu.CompilerParams(vmem_limit_bytes=BIG),
        name="spread_sum",
    )(a, after)


CHUNKS = (
    ("y", 1, 0), ("y", 3, 0), ("d", 0, GRP), ("y", 2, 0),
)


def near_kernel(pos, near_x, near_dy, y_own, wg, wu, wd, ada, d1, d3, acc, low, *refs):
    nx, ny, yv, wgv, wuv, wdv, av, v1, v3, sem = refs
    pairs = ((near_x, nx), (wg, wgv), (wu, wuv), (y_own, yv), (near_dy, ny), (wd, wdv), (ada, av))
    pairs += ((d1, v1), (d3, v3))
    copies = fetch(pairs, sem)
    at = pl.ds(pl.multiple_of(Y_BASE + pos[2] * Y_WIDE, 128), Y_WIDE)
    copies[0].wait()
    copies[1].wait()
    acc[0, :GRP] = nn(nx[...], wgv[...])
    copies[2].wait()
    acc[1, :GRP] = nn(nx[...], wuv[...])
    copies[3].wait()
    acc[0, GRP:] = nn(yv[:, :Y_WIDE], wgv[at, :])
    acc[1, GRP:] = nn(yv[:, :Y_WIDE], wuv[at, :])
    copies[4].wait()
    copies[5].wait()
    acc[2, :GRP] = nt(ny[...], wdv[...])
    acc[2, GRP:] = nt(yv[:, Y_WIDE:], wdv[:, at])
    copies[6].wait()
    low[:GRP, :128] = nn(nx[...], av[:, :128])
    low[:GRP, 128:] = nn(ny[...], av[:, 128:])
    low[GRP:, :128] = nn(yv[:, :Y_WIDE], av[at, :128])
    low[GRP:, 128:] = nn(yv[:, Y_WIDE:], av[at, 128:])
    for i, (v, r) in enumerate(((v1, 1), (v3, 3))):
        copies[7 + i].wait()
        rows = slice(r * GRP, (r + 1) * GRP)
        xs, dys = v[:, :D_WIDE], v[:, D_WIDE : 2 * D_WIDE]
        acc[0, rows] += nn(xs, wgv[D_BASE:, :])
        acc[1, rows] += nn(xs, wuv[D_BASE:, :])
        acc[2, rows] += nt(dys, wdv[:, D_BASE:])
        low[rows, :128] += nn(xs, av[D_BASE:, :128])
        low[rows, 128:] += nn(dys, av[D_BASE:, 128:])


def near_product(pos, near_x, near_dy, y_own, wg, wu, wd, ada, d1, d3):
    whole = (near_x, near_dy, y_own, wg, wu, wd, ada, d1, d3)
    return pl.pallas_call(
        near_kernel,
        out_shape=[shape((3, ROWS, FF), f32), shape((ROWS, 256), f32)],
        in_specs=[INS] + [ANY] * 9,
        out_specs=[INV] * 2,
        scratch_shapes=[VMEM(a.shape, bf16) for a in whole] + [pltpu.SemaphoreType.DMA((9,))],
        compiler_params=pltpu.CompilerParams(vmem_limit_bytes=BIG),
        name="near_product",
    )(pos, *whole)


def main_kernel(pos, *refs):
    n = len(CHUNKS)
    chunks, refs = refs[:n], refs[n:]
    wg, wu, wd, ada, near_acc, near_low, bg, bu, df = refs[:9]
    g_out, hid_out, low_out, side_out, zt, zb, y_out = refs[9:16]
    refs = refs[16:]
    bufs, refs = refs[:n], refs[n:]
    wgv, wuv, wdv, av, acc, low, sem = refs
    pairs = [(wg, wgv), (wu, wuv), (wd, wdv), (ada, av)] + list(zip(chunks, bufs))
    copies = [pltpu.make_async_copy(a, b, sem.at[i]) for i, (a, b) in enumerate(pairs)]
    for copy in copies:
        copy.start()
    acc[...] = near_acc[...]
    low[...] = near_low[...]
    for copy in copies[:4]:
        copy.wait()
    for i, (kind, k, lo) in enumerate(CHUNKS):
        copies[4 + i].wait()
        start, wide = start_of(pos, kind, k)
        at = pl.ds(pl.multiple_of(start, 128), wide)
        rows = slice(GRP + lo, GRP + lo + bufs[i].shape[0])
        xs, dys = bufs[i][:, :wide], bufs[i][:, wide : 2 * wide]
        acc[0, rows] += nn(xs, wgv[at, :])
        acc[1, rows] += nn(xs, wuv[at, :])
        acc[2, rows] += nt(dys, wdv[:, at])
        low[rows, :128] += nn(xs, av[at, :128])
        low[rows, 128:] += nn(dys, av[at, 128:])

    low_out[...] = low[...].astype(bf16)
    lo_g, lo_u, query = low_out[:, :64], low_out[:, 64:128], low_out[:, 128:192]
    gate_pre = acc[0] + SCALE * nn(lo_g, bg[...])
    up_pre = acc[1] + SCALE * nn(lo_u, bu[...])
    back = acc[2]
    sig = 1.0 / (1.0 + jnp.exp(-gate_pre))
    swish = gate_pre * sig
    hidden = (swish * up_pre).astype(bf16)
    grad_hidden = back + SCALE * nt(query, df[...])
    gg = (grad_hidden * up_pre * (sig * (1.0 + gate_pre * (1.0 - sig)))).astype(bf16)
    gu = (grad_hidden * swish).astype(bf16)
    g_out[:, :FF] = gg
    g_out[:, FF:] = gu
    hid_out[...] = hidden

    zi = (pos[1] + NZ // 2) % NZ
    half = NY * HALF // 2
    both = jnp.concatenate([gg, gu], axis=1)

    def stacked(starts):
        at = [pl.ds(pl.multiple_of(i, 32), HALF) for i in starts]
        rows = [jnp.concatenate([wgv[i, :], wuv[i, :]], axis=1) for i in at]
        return nt(jnp.concatenate(rows, axis=0), both).astype(bf16)

    far = stacked([(zi * NY + y) * 192 + HALF for y in range(NY)])
    zt[...] = far[:half]
    zb[...] = far[half:]
    for y in range(NY):
        y_out[y * NZ * HALF : (y + 1) * NZ * HALF] = stacked(
            [(z * NY + y) * 192 for z in range(NZ)]
        )
    side_down = nn(hidden, df[...])
    score = jnp.sum(back * hidden.astype(f32), axis=1, keepdims=True) + SCALE * jnp.sum(
        query.astype(f32) * side_down, axis=1, keepdims=True
    )
    side_out[:ROWS, :64] = nt(gg, bg[...]).astype(bf16)
    side_out[:ROWS, 64:128] = nt(gu, bu[...]).astype(bf16)
    side_out[:ROWS, 128:192] = side_down.astype(bf16)
    side_out[:ROWS, 192:] = jnp.broadcast_to(score, (ROWS, 64)).astype(bf16)
    side_out[ROWS:] = jnp.zeros((512 - ROWS, 256), bf16)


def main_product(pos, chunks, wg, wu, wd, ada, near_acc, near_low, bg, bu, df):
    scratch = [VMEM(c.shape, bf16) for c in (*chunks, wg, wu, wd, ada)]
    scratch += [VMEM((3, ROWS, FF), f32), VMEM((ROWS, 256), f32)]
    scratch += [pltpu.SemaphoreType.DMA((len(chunks) + 4,))]
    out = [shape((ROWS, 2 * FF)), shape((ROWS, FF)), shape((ROWS, 256)), shape((512, 256))]
    out += [shape((NY * HALF // 2, ROWS))] * 2 + [shape((NY * NZ * HALF, ROWS))]
    return pl.pallas_call(
        main_kernel,
        out_shape=out,
        in_specs=[INS] + [ANY] * (len(chunks) + 4) + [INV] * 5,
        out_specs=[INV] * len(out),
        scratch_shapes=scratch,
        compiler_params=pltpu.CompilerParams(vmem_limit_bytes=BIG),
        name="main_product",
    )(pos, *chunks, wg, wu, wd, ada, near_acc, near_low, bg, bu, df)


def terms_kernel(wg4, wu4, g, out, wgv, wuv, sem):
    copies = []
    for z in range(NZ):
        for i, (a, b) in enumerate(((wg4, wgv), (wu4, wuv))):
            src = a.at[z, :, pl.ds(HALF, HALF), :]
            copies.append(pltpu.make_async_copy(src, b.at[z], sem.at[2 * z + i]))
            copies[-1].start()
    gg, gu = g[:, :FF], g[:, FF:]
    for z in range(NZ):
        copies[2 * z].wait()
        copies[2 * z + 1].wait()
        a, b = wgv[z].reshape(NY * HALF, FF), wuv[z].reshape(NY * HALF, FF)
        out[z] = (nt(a, gg) + nt(b, gu)).astype(bf16)


def z_terms(wg, wu, g):
    four = (NZ, NY, 192, FF)
    return pl.pallas_call(
        terms_kernel,
        out_shape=shape((NZ, NY * HALF, ROWS)),
        in_specs=[ANY] * 2 + [INV],
        out_specs=INV,
        scratch_shapes=[VMEM((NZ, NY, HALF, FF), bf16)] * 2 + [pltpu.SemaphoreType.DMA((2 * NZ,))],
        compiler_params=pltpu.CompilerParams(vmem_limit_bytes=BIG),
        name="z_terms",
    )(wg.reshape(four), wu.reshape(four), g)


def step_kernel(halved, idx, up_term, down_term, fore, aft, *refs):
    up, down = refs[-2:]
    half = up.shape[0] // 2
    u, v = up_term[0].astype(f32), down_term[0].astype(f32)
    if halved:
        up[:half] = (u[:half] + fore[...].astype(f32)).astype(bf16)
        up[half:] = up_term[0, half:]
        down[:half] = down_term[0, :half]
        down[half:] = (v[half:] + aft[...].astype(f32)).astype(bf16)
    else:
        up[...] = (u + fore[...].astype(f32)).astype(bf16)
        down[...] = (v + aft[...].astype(f32)).astype(bf16)


def last_kernel(idx, term, fore, aft, *refs):
    refs[-1][...] = (term[0].astype(f32) + fore[...].astype(f32) + aft[...].astype(f32)).astype(bf16)


def whole(a):
    return pl.BlockSpec(a.shape, lambda i, idx, n=len(a.shape): (0,) * n)


def term_block(terms, k):
    return pl.BlockSpec((1, *terms.shape[1:]), lambda i, idx: (idx[k], 0, 0))


def scatter_step(kernel, idx, which, terms, fore, aft, after, hand=None):
    out = [shape(terms.shape[1:])] * len(which)
    in_specs = [term_block(terms, k % NZ) for k in which] + [whole(fore), whole(aft)]
    in_specs += [ANY] * len(after)
    out_specs = [whole(o) for o in out]
    args, alias = (idx, *[terms] * len(which), fore, aft, *after), {}
    if hand is not None:
        alias = {len(args): len(out)}
        in_specs, out_specs = in_specs + [ANY], out_specs + [ANY]
        args, out = (*args, hand), out + [shape(hand.shape)]
    spec = pltpu.PrefetchScalarGridSpec(
        num_scalar_prefetch=1, grid=(1,), in_specs=in_specs, out_specs=out_specs
    )
    return pl.pallas_call(
        kernel,
        out_shape=out,
        grid_spec=spec,
        input_output_aliases=alias,
        compiler_params=pltpu.CompilerParams(vmem_limit_bytes=BIG),
        name="scatter_step",
    )(*args)


def z_scatter(idx, top, bottom, terms, after):
    fore, aft = over_dp(top, z_perm(1)), over_dp(bottom, z_perm(-1))
    for k in range(NZ // 2 - 1, 0, -1):
        kernel = functools.partial(step_kernel, k == NZ // 2 - 1)
        up, down = scatter_step(kernel, idx, (k, -k), terms, fore, aft, after[k])
        fore, aft = over_dp(up, z_perm(1)), over_dp(down, z_perm(-1))
    return scatter_step(last_kernel, idx, (0,), terms, fore, aft, after[0])[0]


Z_GROUPS = [[z * NY + y for z in range(NZ)] for y in range(NY)]
Y_GROUPS = [[z * NY + y for y in range(NY)] for z in range(NZ)]


def swap(a, groups):
    return lax.all_to_all(a, "dp", 0, 0, axis_index_groups=groups, tiled=True)


def sum_kernel(a, out):
    total = a[0].astype(f32)
    for k in range(1, a.shape[0]):
        total = total + a[k].astype(f32)
    out[...] = total.astype(out.dtype)


def sum_first(a, kind):
    return pl.pallas_call(
        sum_kernel,
        out_shape=shape(a.shape[1:], kind),
        in_specs=[INV],
        out_specs=INV,
        compiler_params=pltpu.CompilerParams(vmem_limit_bytes=BIG),
        name="sum_first",
    )(a)


def trade(a):
    return lax.all_to_all(a, "dp", 0, 0, tiled=True)


def body(
    tokens,
    cotangent,
    routes,
    router_gate_weight,
    frozen_gate_weight,
    frozen_up_weight,
    frozen_down_weight,
    gate_adapter_first,
    gate_adapter_second,
    up_adapter_first,
    up_adapter_second,
    down_adapter_first,
    down_adapter_second,
):
    d = lax.axis_index("dp")
    e = lax.axis_index("expert")
    z, y = d // NY, d % NY
    x, c = e // NC, e % NC
    pos = jnp.stack([d, z, y, x, c]).astype(jnp.int32)
    rows_dev = tokens.shape[0]
    wg, wu, wd = frozen_gate_weight[0], frozen_up_weight[0], frozen_down_weight[0]
    a_gate, a_up, d_second = gate_adapter_first[0], up_adapter_first[0], down_adapter_second[0]
    b_gate, b_up, d_first = gate_adapter_second[0], up_adapter_second[0], down_adapter_first[0]

    adapters = jnp.concatenate([a_gate, a_up, d_second.T, jnp.zeros_like(a_gate)], axis=1)
    adapters = lax.all_gather(adapters, "dp", axis=0, tiled=True)

    tok_p, cot_p = over_expert(tokens, CORE), over_expert(cotangent, CORE)
    info = jnp.concatenate([routes.astype(f32), router_gate_weight.astype(f32)], axis=1).T
    info_p = over_expert(info, CORE)
    placed = place_rows(pos, info, info_p, tokens, tok_p, cotangent, cot_p)
    near_x, near_dy, near_own, place, first = placed[6:]

    def exchange(parts):
        return [over_expert(p, x_perm(r + 1)) for r, p in enumerate(parts)]

    ring_got = exchange(placed[0:3])
    y_own, *d_msg = join_rows(ring_got, placed[3:6])
    d_got = exchange(d_msg)
    by = {}
    near_acc, near_low = near_product(
        pos, near_x, near_dy, y_own, wg, wu, wd, adapters, d_got[0], d_got[2]
    )
    for k in (1, 2, 3):
        by["y", k] = over_dp(y_own, y_perm(-k))
    n_dp = NZ * NY
    chunks = [d_got[lo // GRP] if kind == "d" else by[kind, k] for kind, k, lo in CHUNKS]
    g, hidden, low, side_part, zt, zb, y_far = main_product(
        pos, chunks, wg, wu, wd, adapters, near_acc, near_low, b_gate, b_up, d_first
    )
    own = jnp.concatenate([near_own] + [m[:, 2 * D_WIDE :] for m in d_got], axis=0)
    x_own, dy_own = own[:, :256], own[:, 256:]
    low_gate, low_up, query = low[:, :64], low[:, 64:128], low[:, 128:192]
    grad_gate, grad_up = g[:, :FF], g[:, FF:]
    terms = z_terms(wg, wu, g)
    idx = (z + jnp.arange(NZ, dtype=jnp.int32)) % NZ
    side_got = trade(side_part.reshape(n_dp, 512 // n_dp, 256))
    sides = trade(spread_sum(side_got, zt)).reshape(512, 256)
    upper = y_far
    for groups in (Y_GROUPS, Z_GROUPS):
        upper = lax.psum_scatter(
            upper, "dp", scatter_dimension=0, axis_index_groups=groups, tiled=True
        )
    upper = upper.astype(f32)
    after = {3: (), 2: (side_got,), 1: (), 0: (sides,)}
    after_z = z_scatter(idx, zt, zb, terms, after).reshape(NY, HALF, ROWS)
    lower = sum_first(swap(after_z, Y_GROUPS), f32)
    sides = sides[:ROWS]
    a_both = jnp.concatenate([a_gate, a_up], axis=1)
    both_sides, side_down = sides[:, :128], sides[:, 128:192]

    summed = jnp.concatenate([upper, lower], axis=0) + SCALE * dot(a_both, both_sides, 1, 1)
    final = jnp.concatenate(
        [summed.astype(bf16), jnp.broadcast_to(sides[:, 192][None], (16, ROWS))], axis=0
    )
    parts = [final[:, :GRP]] + [
        over_expert(final[:, r * GRP : (r + 1) * GRP], x_perm(-r)) for r in (1, 2, 3)
    ]
    out = None
    for r, part in enumerate(parts):
        lo, hi = r * GRP, (r + 1) * GRP
        term = (
            dot(part[:192], place[lo:hi], 1, 0),
            dot(part[192:], first[lo:hi], 1, 0)[:8],
            dot(part[192:], place[lo:hi] - first[lo:hi], 1, 0)[:8],
        )
        term = jnp.concatenate(term, axis=0)
        out = term if out is None else out + term
    out = out[:, :rows_dev] + over_expert(out[:, rows_dev:], CORE)
    input_grad = out[:192].T.astype(bf16)
    gate_grad = jnp.stack([out[192], out[200]], axis=1) / router_gate_weight.astype(f32)

    grad_a_gate = SCALE * dot(x_own, both_sides[:, :64], 0, 0)[:192]
    grad_a_up = SCALE * dot(x_own, both_sides[:, 64:], 0, 0)[:192]
    grad_b_gate = SCALE * dot(low_gate, grad_gate, 0, 0)
    grad_b_up = SCALE * dot(low_up, grad_up, 0, 0)
    grad_a_down = SCALE * dot(hidden, query, 0, 0)
    grad_b_down = SCALE * dot(side_down, dy_own, 0, 0)[:, :192]
    return (
        input_grad,
        gate_grad,
        grad_a_gate.astype(bf16)[None],
        grad_b_gate.astype(bf16)[None],
        grad_a_up.astype(bf16)[None],
        grad_b_up.astype(bf16)[None],
        grad_a_down.astype(bf16)[None],
        grad_b_down.astype(bf16)[None],
    )


def solution(mesh):
    return jax.shard_map(
        body,
        mesh=mesh,
        in_specs=(
            P("expert", None),
            P("expert", None),
            P("expert", None),
            P("expert", None),
            P("expert", None, "dp"),
            P("expert", None, "dp"),
            P("expert", "dp", None),
            P("expert", "dp", None),
            P("expert", None, "dp"),
            P("expert", "dp", None),
            P("expert", None, "dp"),
            P("expert", "dp", None),
            P("expert", None, "dp"),
        ),
        out_specs=(
            P("expert", "dp"),
            P("expert", None),
            P("expert", "dp", None),
            P("expert", None, "dp"),
            P("expert", "dp", None),
            P("expert", None, "dp"),
            P("expert", "dp", None),
            P("expert", None, "dp"),
        ),
        check_vma=False,
    )
```

```python
import functools

import jax
import jax.numpy as jnp
from jax import lax
from jax.experimental import pallas as pl
from jax.experimental.pallas import tpu as pltpu
from jax.sharding import PartitionSpec as P

NZ, NY, NX, NC = 8, 4, 4, 2
SCALE = 0.25
CAP = 48
GRP = 2 * CAP
Y_BASE, Y_WIDE = 0, 1024
D_BASE, D_WIDE = 4096, 2048
HALF = 96
bf16 = jnp.bfloat16
f32 = jnp.float32


def z_perm(s):
    return [(z * NY + y, ((z + s) % NZ) * NY + y) for z in range(NZ) for y in range(NY)]


def y_perm(s):
    return [(z * NY + y, z * NY + (y + s) % NY) for z in range(NZ) for y in range(NY)]


def x_perm(s):
    return [(x * NC + c, ((x + s) % NX) * NC + c) for x in range(NX) for c in range(NC)]


CORE = [(x * NC + c, x * NC + 1 - c) for x in range(NX) for c in range(NC)]


def over_dp(a, perm):
    return lax.ppermute(a, "dp", perm)


def over_expert(a, perm):
    return lax.ppermute(a, "expert", perm)


def dot(a, b, i, j):
    return lax.dot_general(a, b, (((i,), (j,)), ((), ())), preferred_element_type=f32)


MIB = 1024 * 1024
BIG = 58 * MIB
OWN_AT = 2 * Y_WIDE
ROWS = NX * GRP
FAR = ROWS - GRP
FF = 256
VMEM = pltpu.VMEM
ANY = pl.BlockSpec(memory_space=pl.ANY)
INV = pl.BlockSpec(memory_space=pltpu.VMEM)
INS = pl.BlockSpec(memory_space=pltpu.SMEM)


def shape(dims, kind=bf16):
    return jax.ShapeDtypeStruct(dims, kind)


def lanes(ref, start, wide):
    return ref[:, pl.ds(pl.multiple_of(start, 128), wide)]


def fetch(pairs, sem):
    copies = [pltpu.make_async_copy(a, b, sem.at[i]) for i, (a, b) in enumerate(pairs)]
    for copy in copies:
        copy.start()
    return copies


def slot_rows(sel, own, partner, cols):
    src = jnp.concatenate([own[:, cols], partner[:, cols]], axis=0)
    return jnp.dot(sel, src, preferred_element_type=f32)


def put(refs, at, value):
    value = value.astype(bf16)
    for r in range(3):
        refs[r][:, at : at + value.shape[1]] = value[r * GRP : (r + 1) * GRP]


def place_kernel(pos, info, info_p, tok, tok_p, cot, cot_p, *outs):
    ring_out, d_out = outs[0:3], outs[3:6]
    near_x, near_dy, near_own, place_out, first_out = outs[6:11]
    y_cols, own_cols, wholes, sem = outs[11:15], outs[15:19], outs[19:23], outs[23]
    d, y = pos[0], pos[2]
    odd = d % 2
    y_at = pl.ds(pl.multiple_of(Y_BASE + y * Y_WIDE, 128), Y_WIDE)
    own_at = pl.ds(pl.multiple_of(192 * d - 64 * odd, 128), 256)
    srcs = (tok, tok_p, cot, cot_p)
    copies = fetch(
        [(a.at[:, y_at], b) for a, b in zip(srcs, y_cols)]
        + [(a.at[:, own_at], b) for a, b in zip(srcs, own_cols)]
        + list(zip(srcs, wholes)),
        sem,
    )
    n = tok.shape[0]
    info_all = jnp.concatenate([info[...], info_p[...]], axis=1)
    lane = lax.broadcasted_iota(jnp.int32, (ROWS, 2 * n), 0)
    group = jnp.zeros((ROWS, 2 * n), jnp.int32)
    for k in range(1, NX * NC):
        group = group + jnp.where(lane >= k * CAP, 1, 0)
    slot = (lane - CAP * group).astype(f32)
    block = (group & 1).astype(f32)
    expert = (2 * ((pos[3] + (group >> 1)) & (NX - 1)) + pos[4]).astype(f32)
    ones = jnp.ones((ROWS, 2 * n), f32)
    zeros = jnp.zeros((ROWS, 2 * n), f32)
    token = lax.broadcasted_iota(jnp.int32, (ROWS, 2 * n), 1)
    mine = jnp.where(jnp.where(token >= n, ones, zeros) == block, ones, zeros)
    first = jnp.where(info_all[0:1] == expert, mine, zeros)
    second = jnp.where(info_all[1:2] == expert, mine, zeros)
    row = lax.broadcasted_iota(jnp.int32, (2 * n, 2 * n), 0)
    col = lax.broadcasted_iota(jnp.int32, (2 * n, 2 * n), 1)
    earlier = jnp.where(row < col, 1.0, 0.0).astype(bf16)
    rank = jnp.dot((first + second).astype(bf16), earlier, preferred_element_type=f32)
    first = jnp.where(rank == slot, first, zeros)
    second = jnp.where(rank == slot, second, zeros)
    place = (first + second).astype(bf16)
    weighted = (first * info_all[2:3] + second * info_all[3:4]).astype(bf16)
    place_out[...] = place
    first_out[...] = first.astype(bf16)
    for copy in copies[:8]:
        copy.wait()
    every = slice(None)
    put(ring_out, 0, slot_rows(place[GRP:], y_cols[0], y_cols[1], every))
    put(ring_out, Y_WIDE, slot_rows(weighted[GRP:], y_cols[2], y_cols[3], every))
    for i, sel in enumerate((place, weighted)):
        v = slot_rows(sel, own_cols[2 * i], own_cols[2 * i + 1], every)
        v = jnp.where(odd == 1, pltpu.roll(v, 192, 1), v)
        near_own[:, 256 * i : 256 * i + 256] = v[:GRP].astype(bf16)
        put(d_out, 2 * D_WIDE + 256 * i, v[GRP:])
    for copy in copies[8:]:
        copy.wait()
    step = 512
    for i in range(tok.shape[1] // step):
        cols = slice(i * step, (i + 1) * step)
        for j, (sel, near) in enumerate(((place, near_x), (weighted, near_dy))):
            whole = i * step >= D_BASE
            v = slot_rows(sel if whole else sel[:GRP], wholes[2 * j], wholes[2 * j + 1], cols)
            near[:, cols] = v[:GRP].astype(bf16)
            if whole:
                put(d_out, i * step - D_BASE + j * D_WIDE, v[GRP:])


def place_rows(pos, info, info_p, tok, tok_p, cot, cot_p):
    n = tok.shape[0]
    out = [shape((GRP, OWN_AT))] * 3 + [shape((GRP, 2 * D_WIDE + 512))] * 3
    out += [shape((GRP, tok.shape[1]))] * 2 + [shape((GRP, 512))] + [shape((ROWS, 256))] * 2
    return pl.pallas_call(
        place_kernel,
        out_shape=out,
        in_specs=[INS] + [INV] * 2 + [ANY] * 4,
        out_specs=[INV] * len(out),
        scratch_shapes=[VMEM((n, Y_WIDE), bf16)] * 4
        + [VMEM((n, 256), bf16)] * 4
        + [VMEM(tok.shape, bf16)] * 4
        + [pltpu.SemaphoreType.DMA((12,))],
        compiler_params=pltpu.CompilerParams(vmem_limit_bytes=BIG),
        name="place_rows",
    )(pos, info, info_p, tok, tok_p, cot, cot_p)


def nt(a, b):
    return lax.dot_general(a, b, (((1,), (1,)), ((), ())), preferred_element_type=f32)


def nn(a, b):
    return jnp.dot(a, b, preferred_element_type=f32)


def start_of(pos, kind, k):
    if kind == "y":
        return Y_BASE + ((pos[2] + k + NY) % NY) * Y_WIDE, Y_WIDE
    return D_BASE, D_WIDE


def join_kernel(m1, m2, m3, d1, d2, d3, y_out, o1, o2, o3):
    for r, (m, d, o) in enumerate(((m1, d1, o1), (m2, d2, o2), (m3, d3, o3))):
        y_out[r * GRP : (r + 1) * GRP] = m[...]
        o[...] = d[...]


def join_rows(messages, later):
    return pl.pallas_call(
        join_kernel,
        out_shape=[shape((FAR, OWN_AT))] + [shape(a.shape) for a in later],
        in_specs=[INV] * 6,
        out_specs=[INV] * 4,
        compiler_params=pltpu.CompilerParams(vmem_limit_bytes=BIG),
        name="join_rows",
    )(*messages, *later)


def pack_kernel(ag, au, d2, after, out):
    out[:, :64] = ag[...]
    out[:, 64:128] = au[...]
    out[:, 128:192] = d2[...]
    out[:, 192:] = jnp.zeros((192, 64), bf16)


def pack_adapters(ag, au, d2, after):
    return pl.pallas_call(
        pack_kernel,
        out_shape=shape((192, 256)),
        in_specs=[INV] * 3 + [ANY],
        out_specs=INV,
        compiler_params=pltpu.CompilerParams(vmem_limit_bytes=BIG),
        name="pack_adapters",
    )(ag, au, d2, after)


def spread_kernel(a, after, out):
    total = jnp.sum(a[...].astype(f32), axis=0).astype(bf16)
    for k in range(out.shape[0]):
        out[k] = total


def spread_sum(a, after):
    return pl.pallas_call(
        spread_kernel,
        out_shape=shape(a.shape),
        in_specs=[INV, ANY],
        out_specs=INV,
        compiler_params=pltpu.CompilerParams(vmem_limit_bytes=BIG),
        name="spread_sum",
    )(a, after)


CHUNKS = (
    ("y", 1, 0), ("y", 3, 0), ("d", 0, GRP), ("y", 2, 0),
)


def near_kernel(pos, near_x, near_dy, y_own, wg, wu, wd, ada, d1, d3, acc, low, *refs):
    nx, ny, yv, wgv, wuv, wdv, av, v1, v3, sem = refs
    pairs = ((near_x, nx), (wg, wgv), (wu, wuv), (y_own, yv), (near_dy, ny), (wd, wdv), (ada, av))
    pairs += ((d1, v1), (d3, v3))
    copies = fetch(pairs, sem)
    at = pl.ds(pl.multiple_of(Y_BASE + pos[2] * Y_WIDE, 128), Y_WIDE)
    copies[0].wait()
    copies[1].wait()
    acc[0, :GRP] = nn(nx[...], wgv[...])
    copies[2].wait()
    acc[1, :GRP] = nn(nx[...], wuv[...])
    copies[3].wait()
    acc[0, GRP:] = nn(yv[:, :Y_WIDE], wgv[at, :])
    acc[1, GRP:] = nn(yv[:, :Y_WIDE], wuv[at, :])
    copies[4].wait()
    copies[5].wait()
    acc[2, :GRP] = nt(ny[...], wdv[...])
    acc[2, GRP:] = nt(yv[:, Y_WIDE:], wdv[:, at])
    copies[6].wait()
    low[:GRP, :128] = nn(nx[...], av[:, :128])
    low[:GRP, 128:] = nn(ny[...], av[:, 128:])
    low[GRP:, :128] = nn(yv[:, :Y_WIDE], av[at, :128])
    low[GRP:, 128:] = nn(yv[:, Y_WIDE:], av[at, 128:])
    for i, (v, r) in enumerate(((v1, 1), (v3, 3))):
        copies[7 + i].wait()
        rows = slice(r * GRP, (r + 1) * GRP)
        xs, dys = v[:, :D_WIDE], v[:, D_WIDE : 2 * D_WIDE]
        acc[0, rows] += nn(xs, wgv[D_BASE:, :])
        acc[1, rows] += nn(xs, wuv[D_BASE:, :])
        acc[2, rows] += nt(dys, wdv[:, D_BASE:])
        low[rows, :128] += nn(xs, av[D_BASE:, :128])
        low[rows, 128:] += nn(dys, av[D_BASE:, 128:])


def near_product(pos, near_x, near_dy, y_own, wg, wu, wd, ada, d1, d3):
    whole = (near_x, near_dy, y_own, wg, wu, wd, ada, d1, d3)
    return pl.pallas_call(
        near_kernel,
        out_shape=[shape((3, ROWS, FF), f32), shape((ROWS, 256), f32)],
        in_specs=[INS] + [ANY] * 9,
        out_specs=[INV] * 2,
        scratch_shapes=[VMEM(a.shape, bf16) for a in whole] + [pltpu.SemaphoreType.DMA((9,))],
        compiler_params=pltpu.CompilerParams(vmem_limit_bytes=BIG),
        name="near_product",
    )(pos, *whole)


def main_kernel(pos, *refs):
    n = len(CHUNKS)
    chunks, refs = refs[:n], refs[n:]
    wg, wu, wd, ada, near_acc, near_low, bg, bu, df = refs[:9]
    g_out, hid_out, low_out, side_out, zt, zb, y_out = refs[9:16]
    refs = refs[16:]
    bufs, refs = refs[:n], refs[n:]
    wgv, wuv, wdv, av, acc, low, sem = refs
    pairs = [(wg, wgv), (wu, wuv), (wd, wdv), (ada, av)] + list(zip(chunks, bufs))
    copies = [pltpu.make_async_copy(a, b, sem.at[i]) for i, (a, b) in enumerate(pairs)]
    for copy in copies:
        copy.start()
    acc[...] = near_acc[...]
    low[...] = near_low[...]
    for copy in copies[:4]:
        copy.wait()
    for i, (kind, k, lo) in enumerate(CHUNKS):
        copies[4 + i].wait()
        start, wide = start_of(pos, kind, k)
        at = pl.ds(pl.multiple_of(start, 128), wide)
        rows = slice(GRP + lo, GRP + lo + bufs[i].shape[0])
        xs, dys = bufs[i][:, :wide], bufs[i][:, wide : 2 * wide]
        acc[0, rows] += nn(xs, wgv[at, :])
        acc[1, rows] += nn(xs, wuv[at, :])
        acc[2, rows] += nt(dys, wdv[:, at])
        low[rows, :128] += nn(xs, av[at, :128])
        low[rows, 128:] += nn(dys, av[at, 128:])

    low_out[...] = low[...].astype(bf16)
    lo_g, lo_u, query = low_out[:, :64], low_out[:, 64:128], low_out[:, 128:192]
    gate_pre = acc[0] + SCALE * nn(lo_g, bg[...])
    up_pre = acc[1] + SCALE * nn(lo_u, bu[...])
    back = acc[2]
    sig = 1.0 / (1.0 + jnp.exp(-gate_pre))
    swish = gate_pre * sig
    hidden = (swish * up_pre).astype(bf16)
    grad_hidden = back + SCALE * nt(query, df[...])
    gg = (grad_hidden * up_pre * (sig * (1.0 + gate_pre * (1.0 - sig)))).astype(bf16)
    gu = (grad_hidden * swish).astype(bf16)
    g_out[:, :FF] = gg
    g_out[:, FF:] = gu
    hid_out[...] = hidden

    zi = (pos[1] + NZ // 2) % NZ
    half = NY * HALF // 2
    both = jnp.concatenate([gg, gu], axis=1)

    def stacked(starts):
        at = [pl.ds(pl.multiple_of(i, 32), HALF) for i in starts]
        rows = [jnp.concatenate([wgv[i, :], wuv[i, :]], axis=1) for i in at]
        return nt(jnp.concatenate(rows, axis=0), both).astype(bf16)

    far = stacked([(zi * NY + y) * 192 + HALF for y in range(NY)])
    zt[...] = far[:half]
    zb[...] = far[half:]
    for y in range(NY):
        y_out[y * NZ * HALF : (y + 1) * NZ * HALF] = stacked(
            [(z * NY + y) * 192 for z in range(NZ)]
        )
    side_down = nn(hidden, df[...])
    score = jnp.sum(back * hidden.astype(f32), axis=1, keepdims=True) + SCALE * jnp.sum(
        query.astype(f32) * side_down, axis=1, keepdims=True
    )
    side_out[:ROWS, :64] = nt(gg, bg[...]).astype(bf16)
    side_out[:ROWS, 64:128] = nt(gu, bu[...]).astype(bf16)
    side_out[:ROWS, 128:192] = side_down.astype(bf16)
    side_out[:ROWS, 192:] = jnp.broadcast_to(score, (ROWS, 64)).astype(bf16)
    side_out[ROWS:] = jnp.zeros((512 - ROWS, 256), bf16)


def main_product(pos, chunks, wg, wu, wd, ada, near_acc, near_low, bg, bu, df):
    scratch = [VMEM(c.shape, bf16) for c in (*chunks, wg, wu, wd, ada)]
    scratch += [VMEM((3, ROWS, FF), f32), VMEM((ROWS, 256), f32)]
    scratch += [pltpu.SemaphoreType.DMA((len(chunks) + 4,))]
    out = [shape((ROWS, 2 * FF)), shape((ROWS, FF)), shape((ROWS, 256)), shape((512, 256))]
    out += [shape((NY * HALF // 2, ROWS))] * 2 + [shape((NY * NZ * HALF, ROWS))]
    return pl.pallas_call(
        main_kernel,
        out_shape=out,
        in_specs=[INS] + [ANY] * (len(chunks) + 4) + [INV] * 5,
        out_specs=[INV] * len(out),
        scratch_shapes=scratch,
        compiler_params=pltpu.CompilerParams(vmem_limit_bytes=BIG),
        name="main_product",
    )(pos, *chunks, wg, wu, wd, ada, near_acc, near_low, bg, bu, df)


def terms_kernel(wg4, wu4, g, out, wgv, wuv, sem):
    copies = []
    for z in range(NZ):
        for i, (a, b) in enumerate(((wg4, wgv), (wu4, wuv))):
            src = a.at[z, :, pl.ds(HALF, HALF), :]
            copies.append(pltpu.make_async_copy(src, b.at[z], sem.at[2 * z + i]))
            copies[-1].start()
    gg, gu = g[:, :FF], g[:, FF:]
    for z in range(NZ):
        copies[2 * z].wait()
        copies[2 * z + 1].wait()
        a, b = wgv[z].reshape(NY * HALF, FF), wuv[z].reshape(NY * HALF, FF)
        out[z] = (nt(a, gg) + nt(b, gu)).astype(bf16)


def z_terms(wg, wu, g):
    four = (NZ, NY, 192, FF)
    return pl.pallas_call(
        terms_kernel,
        out_shape=shape((NZ, NY * HALF, ROWS)),
        in_specs=[ANY] * 2 + [INV],
        out_specs=INV,
        scratch_shapes=[VMEM((NZ, NY, HALF, FF), bf16)] * 2 + [pltpu.SemaphoreType.DMA((2 * NZ,))],
        compiler_params=pltpu.CompilerParams(vmem_limit_bytes=BIG),
        name="z_terms",
    )(wg.reshape(four), wu.reshape(four), g)


def step_kernel(halved, idx, up_term, down_term, fore, aft, *refs):
    up, down = refs[-2:]
    half = up.shape[0] // 2
    u, v = up_term[0].astype(f32), down_term[0].astype(f32)
    if halved:
        up[:half] = (u[:half] + fore[...].astype(f32)).astype(bf16)
        up[half:] = up_term[0, half:]
        down[:half] = down_term[0, :half]
        down[half:] = (v[half:] + aft[...].astype(f32)).astype(bf16)
    else:
        up[...] = (u + fore[...].astype(f32)).astype(bf16)
        down[...] = (v + aft[...].astype(f32)).astype(bf16)


def last_kernel(idx, term, fore, aft, *refs):
    refs[-1][...] = (term[0].astype(f32) + fore[...].astype(f32) + aft[...].astype(f32)).astype(bf16)


def whole(a):
    return pl.BlockSpec(a.shape, lambda i, idx, n=len(a.shape): (0,) * n)


def term_block(terms, k):
    return pl.BlockSpec((1, *terms.shape[1:]), lambda i, idx: (idx[k], 0, 0))


def scatter_step(kernel, idx, which, terms, fore, aft, after, hand=None):
    out = [shape(terms.shape[1:])] * len(which)
    in_specs = [term_block(terms, k % NZ) for k in which] + [whole(fore), whole(aft)]
    in_specs += [ANY] * len(after)
    out_specs = [whole(o) for o in out]
    args, alias = (idx, *[terms] * len(which), fore, aft, *after), {}
    if hand is not None:
        alias = {len(args): len(out)}
        in_specs, out_specs = in_specs + [ANY], out_specs + [ANY]
        args, out = (*args, hand), out + [shape(hand.shape)]
    spec = pltpu.PrefetchScalarGridSpec(
        num_scalar_prefetch=1, grid=(1,), in_specs=in_specs, out_specs=out_specs
    )
    return pl.pallas_call(
        kernel,
        out_shape=out,
        grid_spec=spec,
        input_output_aliases=alias,
        compiler_params=pltpu.CompilerParams(vmem_limit_bytes=BIG),
        name="scatter_step",
    )(*args)


def z_scatter(idx, top, bottom, terms, after):
    fore, aft = over_dp(top, z_perm(1)), over_dp(bottom, z_perm(-1))
    for k in range(NZ // 2 - 1, 0, -1):
        kernel = functools.partial(step_kernel, k == NZ // 2 - 1)
        up, down = scatter_step(kernel, idx, (k, -k), terms, fore, aft, after[k])
        fore, aft = over_dp(up, z_perm(1)), over_dp(down, z_perm(-1))
    return scatter_step(last_kernel, idx, (0,), terms, fore, aft, after[0])[0]


Z_GROUPS = [[z * NY + y for z in range(NZ)] for y in range(NY)]
Y_GROUPS = [[z * NY + y for y in range(NY)] for z in range(NZ)]


def swap(a, groups):
    return lax.all_to_all(a, "dp", 0, 0, axis_index_groups=groups, tiled=True)


def sum_kernel(a, out):
    total = a[0].astype(f32)
    for k in range(1, a.shape[0]):
        total = total + a[k].astype(f32)
    out[...] = total.astype(out.dtype)


def sum_first(a, kind):
    return pl.pallas_call(
        sum_kernel,
        out_shape=shape(a.shape[1:], kind),
        in_specs=[INV],
        out_specs=INV,
        compiler_params=pltpu.CompilerParams(vmem_limit_bytes=BIG),
        name="sum_first",
    )(a)


def trade(a):
    return lax.all_to_all(a, "dp", 0, 0, tiled=True)


def body(
    tokens,
    cotangent,
    routes,
    router_gate_weight,
    frozen_gate_weight,
    frozen_up_weight,
    frozen_down_weight,
    gate_adapter_first,
    gate_adapter_second,
    up_adapter_first,
    up_adapter_second,
    down_adapter_first,
    down_adapter_second,
):
    d = lax.axis_index("dp")
    e = lax.axis_index("expert")
    z, y = d // NY, d % NY
    x, c = e // NC, e % NC
    pos = jnp.stack([d, z, y, x, c]).astype(jnp.int32)
    rows_dev = tokens.shape[0]
    wg, wu, wd = frozen_gate_weight[0], frozen_up_weight[0], frozen_down_weight[0]
    a_gate, a_up, d_second = gate_adapter_first[0], up_adapter_first[0], down_adapter_second[0]
    b_gate, b_up, d_first = gate_adapter_second[0], up_adapter_second[0], down_adapter_first[0]

    tok_p, cot_p = over_expert(tokens, CORE), over_expert(cotangent, CORE)
    info = jnp.concatenate([routes.astype(f32), router_gate_weight.astype(f32)], axis=1).T
    info_p = over_expert(info, CORE)
    placed = place_rows(pos, info, info_p, tokens, tok_p, cotangent, cot_p)
    own_adapters = pack_adapters(a_gate, a_up, d_second.T, placed[0])
    adapters = [own_adapters] + [over_dp(own_adapters, y_perm(-k)) for k in (1, 2, 3)]
    adapters = jnp.roll(jnp.stack(adapters), y, axis=0).reshape(NY * 192, 256)
    adapters = lax.all_gather(adapters, "dp", axis=0, axis_index_groups=Z_GROUPS, tiled=True)
    near_x, near_dy, near_own, place, first = placed[6:]

    def exchange(parts):
        return [over_expert(p, x_perm(r + 1)) for r, p in enumerate(parts)]

    ring_got = exchange(placed[0:3])
    y_own, *d_msg = join_rows(ring_got, placed[3:6])
    d_got = exchange(d_msg)
    by = {}
    near_acc, near_low = near_product(
        pos, near_x, near_dy, y_own, wg, wu, wd, adapters, d_got[0], d_got[2]
    )
    for k in (1, 2, 3):
        by["y", k] = over_dp(y_own, y_perm(-k))
    n_dp = NZ * NY
    chunks = [d_got[lo // GRP] if kind == "d" else by[kind, k] for kind, k, lo in CHUNKS]
    g, hidden, low, side_part, zt, zb, y_far = main_product(
        pos, chunks, wg, wu, wd, adapters, near_acc, near_low, b_gate, b_up, d_first
    )
    own = jnp.concatenate([near_own] + [m[:, 2 * D_WIDE :] for m in d_got], axis=0)
    x_own, dy_own = own[:, :256], own[:, 256:]
    low_gate, low_up, query = low[:, :64], low[:, 64:128], low[:, 128:192]
    grad_gate, grad_up = g[:, :FF], g[:, FF:]
    terms = z_terms(wg, wu, g)
    idx = (z + jnp.arange(NZ, dtype=jnp.int32)) % NZ
    side_got = trade(side_part.reshape(n_dp, 512 // n_dp, 256))
    sides = trade(spread_sum(side_got, zt)).reshape(512, 256)
    upper = y_far
    for groups in (Y_GROUPS, Z_GROUPS):
        upper = lax.psum_scatter(
            upper, "dp", scatter_dimension=0, axis_index_groups=groups, tiled=True
        )
    upper = upper.astype(f32)
    after = {3: (), 2: (side_got,), 1: (), 0: (sides,)}
    after_z = z_scatter(idx, zt, zb, terms, after).reshape(NY, HALF, ROWS)
    lower = sum_first(swap(after_z, Y_GROUPS), f32)
    sides = sides[:ROWS]
    a_both = jnp.concatenate([a_gate, a_up], axis=1)
    both_sides, side_down = sides[:, :128], sides[:, 128:192]

    summed = jnp.concatenate([upper, lower], axis=0) + SCALE * dot(a_both, both_sides, 1, 1)
    final = jnp.concatenate(
        [summed.astype(bf16), jnp.broadcast_to(sides[:, 192][None], (16, ROWS))], axis=0
    )
    parts = [final[:, :GRP]] + [
        over_expert(final[:, r * GRP : (r + 1) * GRP], x_perm(-r)) for r in (1, 2, 3)
    ]
    out = None
    for r, part in enumerate(parts):
        lo, hi = r * GRP, (r + 1) * GRP
        term = (
            dot(part[:192], place[lo:hi], 1, 0),
            dot(part[192:], first[lo:hi], 1, 0)[:8],
            dot(part[192:], place[lo:hi] - first[lo:hi], 1, 0)[:8],
        )
        term = jnp.concatenate(term, axis=0)
        out = term if out is None else out + term
    out = out[:, :rows_dev] + over_expert(out[:, rows_dev:], CORE)
    input_grad = out[:192].T.astype(bf16)
    gate_grad = jnp.stack([out[192], out[200]], axis=1) / router_gate_weight.astype(f32)

    grad_a_gate = SCALE * dot(x_own, both_sides[:, :64], 0, 0)[:192]
    grad_a_up = SCALE * dot(x_own, both_sides[:, 64:], 0, 0)[:192]
    grad_b_gate = SCALE * dot(low_gate, grad_gate, 0, 0)
    grad_b_up = SCALE * dot(low_up, grad_up, 0, 0)
    grad_a_down = SCALE * dot(hidden, query, 0, 0)
    grad_b_down = SCALE * dot(side_down, dy_own, 0, 0)[:, :192]
    return (
        input_grad,
        gate_grad,
        grad_a_gate.astype(bf16)[None],
        grad_b_gate.astype(bf16)[None],
        grad_a_up.astype(bf16)[None],
        grad_b_up.astype(bf16)[None],
        grad_a_down.astype(bf16)[None],
        grad_b_down.astype(bf16)[None],
    )


def solution(mesh):
    return jax.shard_map(
        body,
        mesh=mesh,
        in_specs=(
            P("expert", None),
            P("expert", None),
            P("expert", None),
            P("expert", None),
            P("expert", None, "dp"),
            P("expert", None, "dp"),
            P("expert", "dp", None),
            P("expert", "dp", None),
            P("expert", None, "dp"),
            P("expert", "dp", None),
            P("expert", None, "dp"),
            P("expert", "dp", None),
            P("expert", None, "dp"),
        ),
        out_specs=(
            P("expert", "dp"),
            P("expert", None),
            P("expert", "dp", None),
            P("expert", None, "dp"),
            P("expert", "dp", None),
            P("expert", None, "dp"),
            P("expert", "dp", None),
            P("expert", None, "dp"),
        ),
        check_vma=False,
    )
```
